128 devices in a mesh: rep: 16 (over x, y_lo, core), seq: 8 (over z, y_hi).
Axes of the slice: x: 4, y: 4 (y_hi: 2, y_lo: 2; y = y_hi * 2 + y_lo), z: 4, core: 2. Of those that a mesh axis runs over, the one named last changes fastest.
Arguments:
- context: bfloat16 [16, 1024, 3328], P('rep', 'seq'), may hold values from -6 to 6
- grad_out: bfloat16 [16, 1024, 6656], P('rep', 'seq'), may hold values from -6 to 6
- weight: bfloat16 [16, 6656, 3328], P('rep', 'seq'), may hold values from -6 to 6
- momentum: bfloat16 [16, 6656, 3328], P('rep', 'seq'), may hold values from -3 to 3
- gossip_round: int32 [1], replicated, may hold values from 0 to 4095
Outputs:
- ctx_grad: bfloat16 [16, 1024, 3328], P('rep', 'seq')
- new_weight: bfloat16 [16, 6656, 3328], P('rep', 'seq')
- new_momentum: bfloat16 [16, 6656, 3328], P('rep', 'seq')
The draws below stay inside these ranges and needn't reach their ends.
All inputs are finite; a program needn't handle non-finite values.
Results may differ from the reference program's by a relative error of at most 0.017.
Values may be sent and summed in bfloat16 or wider, within the bound.
No kernel may reach another device: no remote copies, remote signals or barrier semaphores. Data moves between devices by JAX's collectives and lax.ppermute only.
A program may use at most 128 MiB of HBM per device.

```python
import math
import jax
import jax.numpy as jnp
from jax import lax

D = 6656
HD = 3328
TOKENS = 1024
REPS = 16
LOG_REP = 4
N_SEQ = 8


def level_of(key, dims, cuts, smallest, high):
    loudness, own = 1.0, jax.random.fold_in(key, 6)
    for position, shards_of in cuts:
        draws = jnp.exp(jax.random.uniform(jax.random.fold_in(own, position), (shards_of,), jnp.float32, smallest / len(cuts), high / len(cuts)))
        loudness = loudness * jnp.repeat(draws, dims[position] // shards_of).reshape([-1 if axis == position else 1 for axis in range(len(dims))])
    return loudness


def normal_values(key, shape, deviation, limit, split=(), dtype=jnp.bfloat16):
    result = jax.random.normal(key, shape, jnp.float32) * deviation
    if len(split) > 0:
        result = level_of(key, shape, split, -0.22, 0.18) * result
    return jnp.clip(result, min=-limit, max=limit).astype(dtype)


def setup_inputs(seed: int = 0) -> dict:
    streams_of = jax.random.split(jax.random.key(seed), 6)
    context = normal_values(streams_of[0], (REPS, TOKENS, HD), 1.0, 6.0, ((0, 16), (1, 8)))
    grad_out = normal_values(streams_of[1], (REPS, TOKENS, D), 1.0, 6.0, ((0, 16), (1, 8)))
    weight = normal_values(streams_of[2], (REPS, D, HD), 1.0, 6.0, ((0, 16), (1, 8)))
    momentum = normal_values(streams_of[3], (REPS, D, HD), 0.5, 3.0, ((0, 16), (1, 8)))
    gossip_round = jax.random.randint(streams_of[4], (1,), 0, 4096).astype(jnp.int32)
    return {"context": context, "grad_out": grad_out, "weight": weight, "momentum": momentum, "gossip_round": gossip_round}


BETA = 0.9
LEARN = 0.1

def one_group(group_items):
    context, grad_out, weight, momentum = group_items
    factor = 1.0 / math.sqrt(HD)
    weight_grad = jnp.dot(grad_out.T, context, preferred_element_type=jnp.float32) * factor
    block_width = D // N_SEQ
    summed = jnp.zeros((TOKENS, HD), jnp.float32)
    for shard_idx in range(N_SEQ):
        lower = shard_idx * block_width
        upper = lower + block_width
        part_term = jnp.dot(grad_out[:, lower:upper], weight[lower:upper, :], preferred_element_type=jnp.float32) * factor
        rounded = lax.optimization_barrier(part_term.astype(jnp.bfloat16))
        summed = summed + rounded.astype(jnp.float32)
    ctx_grad = summed.astype(jnp.bfloat16)
    moved = (BETA * momentum.astype(jnp.float32) + weight_grad).astype(jnp.bfloat16)
    return (ctx_grad, moved)

def reference(context, grad_out, weight, momentum, gossip_round):
    ctx_grad, moved = lax.map(one_group, (context, grad_out, weight, momentum))
    level = jnp.remainder(gossip_round[0].astype(jnp.int32), jnp.int32(LOG_REP))
    distance = jnp.left_shift(jnp.int32(1), level)
    partner_weight = jnp.roll(weight, distance, axis=0)
    partner_moved = jnp.roll(moved, distance, axis=0)
    mixed_mom = (moved.astype(jnp.float32) + partner_moved.astype(jnp.float32)) * 0.5
    new_weight = ((weight.astype(jnp.float32) + partner_weight.astype(jnp.float32)) * 0.5 - LEARN * mixed_mom).astype(jnp.bfloat16)
    return (ctx_grad, new_weight, mixed_mom.astype(jnp.bfloat16))
```

```python
from functools import partial
import math

import jax
import jax.numpy as jnp
from jax import lax
from jax.experimental import pallas as pl
from jax.experimental.pallas import tpu as pltpu
from jax.sharding import PartitionSpec as P

BETA = 0.9
LEARN = 0.1
UNIT = 256
TILE = 208
ROWS = 64
Z, Y = 4, 2
FREE = pl.CostEstimate(flops=0, bytes_accessed=0, transcendentals=0)
OFFSETS = ((0, 0), (0, 1), (-1, 0), (-1, 1), (1, 0), (1, 1), (2, 0), (2, 1))


def shift_rep(value, steps):
    count = lax.axis_size("rep")
    return lax.ppermute(value, "rep", [(i, (i + steps) % count) for i in range(count)])


def shift_seq(value, dz, dy):
    pairs = []
    for z in range(Z):
        for y in range(Y):
            pairs.append((z * Y + y, (z + dz) % Z * Y + (y + dy) % Y))
    return lax.ppermute(value, "seq", pairs)


def member(me, dz, dy):
    z, y = me // Y, me % Y
    return lax.rem(z + dz + Z, Z) * Y + lax.rem(y + dy, Y)


def after(value, *others):
    return lax.optimization_barrier((value, *others))[0]


def gather_context(c, firsts, seconds):
    across = shift_seq(c, 0, 1)
    up, down = shift_seq(c, 1, 0), shift_seq(c, -1, 0)
    across, up, down, *_ = lax.optimization_barrier((across, up, down, *firsts))
    across_up, across_down = shift_seq(across, 1, 0), shift_seq(across, -1, 0)
    across_up, across_down, up, *_ = lax.optimization_barrier((across_up, across_down, up, *seconds))
    far, across_far = shift_seq(up, 1, 0), shift_seq(across_down, -1, 0)
    return (c, across, up, across_up, down, across_down, far, across_far)


def total(*terms):
    value = terms[0].astype(jnp.float32)
    for term in terms[1:]:
        value = value + term.astype(jnp.float32)
    return value.astype(jnp.bfloat16)


def scatter_sum(parts, firsts):
    part = dict(zip(OFFSETS, parts))
    a = shift_seq(part[2, 0], 1, 0)
    b = shift_seq(part[2, 1], -1, 0)
    u1 = shift_seq(part[1, 1], 1, 0)
    v0 = shift_seq(part[-1, 0], -1, 0)
    u0 = shift_seq(total(part[1, 0], a), 1, 0)
    v1 = shift_seq(total(part[-1, 1], b), -1, 0)
    other = shift_seq(total(part[0, 1], after(u1, *firsts), v1), 0, 1)
    return part[0, 0], u0, v0, other


def part_kernel(factor, order, g_ref, w_ref, *refs):
    out_refs, g_all = refs[:-1], refs[-1]

    @pl.when(pl.program_id(0) == 0)
    def _():
        for k in range(g_ref.shape[0]):
            g_all[k] = g_ref[order[k]].T

    for k, out_ref in enumerate(out_refs):
        product = jnp.dot(g_all[k], w_ref[...], preferred_element_type=jnp.float32)
        out_ref[...] = (product * factor).astype(out_ref.dtype)


def part_blocks(order, g, w, factor):
    n, features, tokens = g.shape
    columns = w.shape[1]
    return pl.pallas_call(
        partial(part_kernel, factor),
        out_shape=(jax.ShapeDtypeStruct((tokens, columns), jnp.bfloat16),) * n,
        grid_spec=pltpu.PrefetchScalarGridSpec(
            num_scalar_prefetch=1,
            grid=(columns // UNIT,),
            in_specs=[
                pl.BlockSpec((n, features, tokens), lambda i, order: (0, 0, 0)),
                pl.BlockSpec((features, UNIT), lambda i, order: (0, i)),
            ],
            out_specs=(pl.BlockSpec((tokens, UNIT), lambda i, order: (0, i)),) * n,
            scratch_shapes=[pltpu.VMEM((n, tokens, features), jnp.bfloat16)],
        ),
        compiler_params=pltpu.CompilerParams(vmem_limit_bytes=24 << 20),
        cost_estimate=FREE,
    )(order, g, w)


def moved_kernel(factor, order, g_ref, mom_ref, *refs):
    context_refs, (out_ref, g_all, rows) = refs[:-3], refs[-3:]
    features, tokens = g_ref.shape[1:]

    @pl.when(pl.program_id(0) == 0)
    def _():
        for k in range(g_ref.shape[0]):
            g_all[:, k * tokens : (k + 1) * tokens] = g_ref[order[k]]

    for k, ref in enumerate(context_refs):
        rows[k * tokens : (k + 1) * tokens, :] = ref[...]

    @pl.loop(0, features // TILE)
    def _(i):
        at = pl.ds(pl.multiple_of(i * TILE, TILE), TILE)
        product = jnp.dot(g_all[at, :], rows[...], preferred_element_type=jnp.float32)
        out_ref[at, :] = (BETA * mom_ref[at, :].astype(jnp.float32) + product * factor).astype(out_ref.dtype)


def moved_chunk(order, g, mom, blocks, factor, start, units):
    n, features, tokens = g.shape
    return pl.pallas_call(
        partial(moved_kernel, factor),
        out_shape=jax.ShapeDtypeStruct((features, units * UNIT), jnp.bfloat16),
        grid_spec=pltpu.PrefetchScalarGridSpec(
            num_scalar_prefetch=1,
            grid=(units,),
            in_specs=[
                pl.BlockSpec((n, features, tokens), lambda i, order: (0, 0, 0)),
                pl.BlockSpec((features, UNIT), lambda i, order: (0, start + i)),
            ]
            + [pl.BlockSpec((tokens, UNIT), lambda i, order: (0, start + i))] * n,
            out_specs=pl.BlockSpec((features, UNIT), lambda i, order: (0, i)),
            scratch_shapes=[
                pltpu.VMEM((features, n * tokens), jnp.bfloat16),
                pltpu.VMEM((n * tokens, UNIT), jnp.bfloat16),
            ],
        ),
        compiler_params=pltpu.CompilerParams(vmem_limit_bytes=24 << 20),
        cost_estimate=FREE,
    )(order, g, mom, *blocks)


def mix_kernel(w_ref, wq_ref, m_ref, mq_ref, *refs):
    nw_ref, nm_ref = refs[-2:]

    @pl.loop(0, w_ref.shape[0] // ROWS)
    def _(i):
        at = pl.ds(pl.multiple_of(i * ROWS, ROWS), ROWS)
        mixed = (m_ref[at, :].astype(jnp.float32) + mq_ref[at, :].astype(jnp.float32)) * 0.5
        both = (w_ref[at, :].astype(jnp.float32) + wq_ref[at, :].astype(jnp.float32)) * 0.5
        nw_ref[at, :] = (both - LEARN * mixed).astype(nw_ref.dtype)
        nm_ref[at, :] = mixed.astype(nm_ref.dtype)


def mix_chunk(w, wq, wq_start, m, mq, outs, start, units):
    features = w.shape[0]

    def at(first):
        return pl.BlockSpec((features, UNIT), lambda j: (0, first + j))

    shape = jax.ShapeDtypeStruct(w.shape, jnp.bfloat16)
    held = () if outs is None else tuple(outs)
    return pl.pallas_call(
        mix_kernel,
        out_shape=(shape, shape),
        grid=(units,),
        in_specs=[at(start), at(wq_start), at(0), at(0)] + [pl.BlockSpec(memory_space=pl.ANY)] * len(held),
        out_specs=(at(start), at(start)),
        input_output_aliases={4 + k: k for k in range(len(held))},
        compiler_params=pltpu.CompilerParams(vmem_limit_bytes=16 << 20),
        cost_estimate=FREE,
    )(w, wq, m, mq, *held)


def step(distance, back, late, chunks, c, g, w, mom):
    factor = 1.0 / math.sqrt(c.shape[1])
    me = lax.axis_index("seq")
    order = jnp.stack([member(me, dz, dy) for dz, dy in OFFSETS]).astype(jnp.int32)
    n = Z * Y

    turned = g.T.reshape(n, g.shape[1] // n, g.shape[0])
    mine = lax.all_to_all(turned, "seq", split_axis=0, concat_axis=0, tiled=True)
    wide = back * UNIT
    if back:
        one = shift_rep(w[:, :wide], -distance)
        wq = shift_rep(w[:, wide:], distance)
        two = shift_rep(one, -distance)
        blocks = gather_context(c, (mine, one), (two,))
        wq_back = shift_rep(two, -distance)
        arrived = (wq, wq_back)
    else:
        blocks = gather_context(c, (mine,), ())
        wq = shift_rep(after(w, mine, blocks[1]) if late else w, distance)
        arrived = (wq,)

    pieces = []
    hops = []
    start = 0
    for units in chunks:
        m = moved_chunk(order, mine, mom, blocks, factor, start, units)
        if start < back:
            hops = [shift_rep(m, -distance)]
            hops.append(shift_rep(hops[0], -distance))
            mq_back = shift_rep(hops[1], -distance)
            held = (wq_back, 0, start, units, m, mq_back)
        else:
            pieces.append((wq, start - back, start, units, m, shift_rep(m, distance)))
        start += units

    parts = part_blocks(order, mine, w, factor)
    computed = [piece[4] for piece in pieces]
    terms = scatter_sum(lax.optimization_barrier((*parts, *computed, *arrived))[: len(parts)], hops[:1])
    last = pieces[-1][-1]
    if back:
        pieces = [(*piece[:-1], after(piece[-1], hop)) for piece, hop in zip(pieces, (*hops, mq_back))]
        pieces.insert(2, held)

    outs = None
    for wq_part, wq_start, start, units, m, mq in pieces:
        outs = mix_chunk(w, wq_part, wq_start, m, mq, outs, start, units)
    ctx_grad = total(*lax.optimization_barrier((*terms, last))[:-1])
    return ctx_grad, outs[0], outs[1]


def local(context, grad_out, weight, momentum, gossip_round):
    level = jnp.remainder(gossip_round[0], 4)
    straight = (2, 4, 4, 3)
    branches = [
        partial(step, 1, 0, True, straight),
        partial(step, 2, 0, True, straight),
        partial(step, 4, 3, False, (3, 4, 3, 3)),
        partial(step, 8, 0, False, straight),
    ]
    outs = lax.switch(level, branches, context[0], grad_out[0], weight[0], momentum[0])
    return tuple(out[None] for out in outs)


def solution(mesh):
    spec = P("rep", "seq", None)
    return jax.shard_map(
        local,
        mesh=mesh,
        in_specs=(spec, spec, spec, spec, P()),
        out_specs=(spec, spec, spec),
        check_vma=False,
    )
```

```python
from functools import partial
import math

import jax
import jax.numpy as jnp
from jax import lax
from jax.experimental import pallas as pl
from jax.experimental.pallas import tpu as pltpu
from jax.sharding import PartitionSpec as P

BETA = 0.9
LEARN = 0.1
UNIT = 256
ROWS = 64
Z, Y = 4, 2
FREE = pl.CostEstimate(flops=0, bytes_accessed=0, transcendentals=0)
OFFSETS = ((0, 0), (0, 1), (-1, 0), (-1, 1), (1, 0), (1, 1), (2, 0), (2, 1))


def shift_rep(value, steps):
    count = lax.axis_size("rep")
    return lax.ppermute(value, "rep", [(i, (i + steps) % count) for i in range(count)])


def shift_seq(value, dz, dy):
    pairs = []
    for z in range(Z):
        for y in range(Y):
            pairs.append((z * Y + y, (z + dz) % Z * Y + (y + dy) % Y))
    return lax.ppermute(value, "seq", pairs)


def member(me, dz, dy):
    z, y = me // Y, me % Y
    return lax.rem(z + dz + Z, Z) * Y + lax.rem(y + dy, Y)


def after(value, *others):
    return lax.optimization_barrier((value, *others))[0]


def gather_context(c, firsts, seconds):
    across = shift_seq(c, 0, 1)
    up, down = shift_seq(c, 1, 0), shift_seq(c, -1, 0)
    across, up, down, *_ = lax.optimization_barrier((across, up, down, *firsts))
    across_up, across_down = shift_seq(across, 1, 0), shift_seq(across, -1, 0)
    across_up, across_down, up, *_ = lax.optimization_barrier((across_up, across_down, up, *seconds))
    far, across_far = shift_seq(up, 1, 0), shift_seq(across_down, -1, 0)
    return (c, across, up, across_up, down, across_down, far, across_far)


def total(*terms):
    value = terms[0].astype(jnp.float32)
    for term in terms[1:]:
        value = value + term.astype(jnp.float32)
    return value.astype(jnp.bfloat16)


def scatter_sum(part, seconds, thirds):
    part = {offset: part[k] for k, offset in enumerate(OFFSETS)}
    a = shift_seq(part[2, 0], 1, 0)
    b = shift_seq(part[2, 1], -1, 0)
    u1 = shift_seq(part[1, 1], 1, 0)
    v0 = shift_seq(part[-1, 0], -1, 0)
    a, b, *_ = lax.optimization_barrier((a, b, *seconds))
    u0 = shift_seq(total(part[1, 0], a), 1, 0)
    v1 = shift_seq(total(part[-1, 1], b), -1, 0)
    u1, v1, *_ = lax.optimization_barrier((u1, v1, *thirds))
    other = shift_seq(total(part[0, 1], u1, v1), 0, 1)
    return part[0, 0], u0, v0, other


def part_kernel(factor, order, g_ref, w_ref, *refs):
    out_refs, g_all = refs[:-1], refs[-1]

    @pl.when(pl.program_id(0) == 0)
    def _():
        for k in range(g_ref.shape[0]):
            g_all[k] = g_ref[order[k]].T

    for k in range(g_ref.shape[0]):
        product = jnp.dot(g_all[k], w_ref[...], preferred_element_type=jnp.float32)
        out_refs[k][...] = (product * factor).astype(w_ref.dtype)


def part_blocks(order, g, w, factor):
    n, features, tokens = g.shape
    columns = w.shape[1]
    return pl.pallas_call(
        partial(part_kernel, factor),
        out_shape=(jax.ShapeDtypeStruct((tokens, columns), jnp.bfloat16),) * n,
        grid_spec=pltpu.PrefetchScalarGridSpec(
            num_scalar_prefetch=1,
            grid=(columns // UNIT,),
            in_specs=[
                pl.BlockSpec((n, features, tokens), lambda i, order: (0, 0, 0)),
                pl.BlockSpec((features, UNIT), lambda i, order: (0, i)),
            ],
            out_specs=(pl.BlockSpec((tokens, UNIT), lambda i, order: (0, i)),) * n,
            scratch_shapes=[pltpu.VMEM((n, tokens, features), jnp.bfloat16)],
        ),
        compiler_params=pltpu.CompilerParams(vmem_limit_bytes=14 << 20),
        cost_estimate=FREE,
    )(order, g, w)


def moved_kernel(factor, chunks, order, g_ref, mom_ref, *refs):
    n, features, tokens = g_ref.shape
    context_refs, out_refs, (g_all, rows) = refs[:n], refs[n:-2], refs[-2:]
    i = pl.program_id(0)

    @pl.when(i == 0)
    def _():
        for k in range(n):
            g_all[:, k * tokens : (k + 1) * tokens] = g_ref[order[k]]

    for k, ref in enumerate(context_refs):
        rows[k * tokens : (k + 1) * tokens, :] = ref[...]
    product = jnp.dot(g_all[...], rows[...], preferred_element_type=jnp.float32)
    value = (BETA * mom_ref[...].astype(jnp.float32) + product * factor).astype(mom_ref.dtype)
    first = 0
    for units, out_ref in zip(chunks, out_refs):

        @pl.when(jnp.logical_and(i >= first, i < first + units))
        def _():
            out_ref[...] = value

        first += units


def moved_chunks(order, g, mom, blocks, factor, start, chunks):
    n, features, tokens = g.shape
    specs = []
    first = 0
    for units in chunks:
        specs.append(
            pl.BlockSpec(
                (features, UNIT),
                lambda i, order, first=first, units=units: (0, jnp.clip(i - first, 0, units - 1)),
            )
        )
        first += units
    return pl.pallas_call(
        partial(moved_kernel, factor, chunks),
        out_shape=tuple(jax.ShapeDtypeStruct((features, units * UNIT), jnp.bfloat16) for units in chunks),
        grid_spec=pltpu.PrefetchScalarGridSpec(
            num_scalar_prefetch=1,
            grid=(first,),
            in_specs=[
                pl.BlockSpec((n, features, tokens), lambda i, order: (0, 0, 0)),
                pl.BlockSpec((features, UNIT), lambda i, order: (0, start + i)),
            ]
            + [pl.BlockSpec((tokens, UNIT), lambda i, order: (0, start + i))] * n,
            out_specs=tuple(specs),
            scratch_shapes=[
                pltpu.VMEM((features, n * tokens), jnp.bfloat16),
                pltpu.VMEM((n * tokens, UNIT), jnp.bfloat16),
            ],
        ),
        compiler_params=pltpu.CompilerParams(vmem_limit_bytes=18 << 20),
        cost_estimate=FREE,
    )(order, g, mom, *blocks)


def mix_kernel(w_ref, wq_ref, m_ref, mq_ref, *refs):
    nw_ref, nm_ref = refs[-2:]

    @pl.loop(0, w_ref.shape[0] // ROWS)
    def _(i):
        at = pl.ds(pl.multiple_of(i * ROWS, ROWS), ROWS)
        mixed = (m_ref[at, :].astype(jnp.float32) + mq_ref[at, :].astype(jnp.float32)) * 0.5
        both = (w_ref[at, :].astype(jnp.float32) + wq_ref[at, :].astype(jnp.float32)) * 0.5
        nw_ref[at, :] = (both - LEARN * mixed).astype(nw_ref.dtype)
        nm_ref[at, :] = mixed.astype(nm_ref.dtype)


def mix_chunk(w, wq, wq_start, m, mq, outs, start, units):
    features = w.shape[0]

    def at(first):
        return pl.BlockSpec((features, UNIT), lambda j: (0, first + j))

    shape = jax.ShapeDtypeStruct(w.shape, jnp.bfloat16)
    held = () if outs is None else tuple(outs)
    return pl.pallas_call(
        mix_kernel,
        out_shape=(shape, shape),
        grid=(units,),
        in_specs=[at(start), at(wq_start), at(0), at(0)] + [pl.BlockSpec(memory_space=pl.ANY)] * len(held),
        out_specs=(at(start), at(start)),
        input_output_aliases={4 + k: k for k in range(len(held))},
        compiler_params=pltpu.CompilerParams(vmem_limit_bytes=8 << 20),
        cost_estimate=FREE,
    )(w, wq, m, mq, *held)


def step(distance, back, idle_y, chunks, c, g, w, mom):
    factor = 1.0 / math.sqrt(c.shape[1])
    me = lax.axis_index("seq")
    order = jnp.stack([member(me, dz, dy) for dz, dy in OFFSETS]).astype(jnp.int32)
    n = Z * Y

    turned = g.T.reshape(n, g.shape[1] // n, g.shape[0])
    mine = lax.all_to_all(turned, "seq", split_axis=0, concat_axis=0, tiled=True)
    part = part_blocks(order, mine, w, factor)
    wide = back * UNIT
    hops = ()
    pieces = []
    if back:
        one = shift_rep(w[:, :wide], -distance)
        wq = shift_rep(w[:, wide:], distance)
        two = shift_rep(one, -distance)
        blocks = gather_context(c, (mine, one), (two, part[0]))
        wq_back = shift_rep(two, -distance)
        (m_back,) = moved_chunks(order, mine, mom, blocks, factor, 0, (back,))
        first = shift_rep(m_back, -distance)
        second = shift_rep(first, -distance)
        mq_back = shift_rep(second, -distance)
        hops = (first, second, mq_back)
        m = moved_chunks(after(order, m_back), mine, mom, blocks, factor, back, chunks)
        part = lax.optimization_barrier((*part, wq, wq_back, m[-1]))[:n]
    else:
        blocks = gather_context(c, (mine,), (part[0],))
        wq = shift_rep(w if idle_y else after(w, mine, blocks[1]), distance)
        m = moved_chunks(order, mine, mom, blocks, factor, 0, chunks)
        part = lax.optimization_barrier((*part, wq, m[-1]))[:n]

    start = 0
    for k, units in enumerate(chunks):
        mq = shift_rep(m[k], distance)
        pieces.append([wq, start, back + start, units, m[k], after(mq, hops[k]) if back else mq])
        start += units
    if back:
        pieces.insert(len(pieces) - 1, [wq_back, 0, 0, back, m_back, mq_back])

    terms = scatter_sum(part, hops[:1], hops[1:2])
    if idle_y:
        ctx_grad = total(*terms)
        pieces[-1][-1] = after(pieces[-1][-1], ctx_grad)
    else:
        ctx_grad = total(*lax.optimization_barrier((*terms, pieces[-1][-1]))[:-1])
    outs = None
    for wq_part, wq_start, start, units, m_part, mq_part in pieces:
        outs = mix_chunk(w, wq_part, wq_start, m_part, mq_part, outs, start, units)
    return ctx_grad, outs[0], outs[1]


def local(context, grad_out, weight, momentum, gossip_round):
    level = jnp.remainder(gossip_round[0], 4)
    straight = (5, 5, 3)
    branches = [
        partial(step, 1, 0, False, straight),
        partial(step, 2, 0, False, straight),
        partial(step, 4, 3, True, (4, 4, 2)),
        partial(step, 8, 0, True, straight),
    ]
    outs = lax.switch(level, branches, context[0], grad_out[0], weight[0], momentum[0])
    return tuple(out[None] for out in outs)


def solution(mesh):
    spec = P("rep", "seq", None)
    return jax.shard_map(
        local,
        mesh=mesh,
        in_specs=(spec, spec, spec, spec, P()),
        out_specs=(spec, spec, spec),
        check_vma=False,
    )
```

```python
from functools import partial
import math

import jax
import jax.numpy as jnp
from jax import lax
from jax.experimental import pallas as pl
from jax.experimental.pallas import tpu as pltpu
from jax.sharding import PartitionSpec as P

BETA = 0.9
LEARN = 0.1
UNIT = 256
ROWS = 64
Z, Y = 4, 2
FREE = pl.CostEstimate(flops=0, bytes_accessed=0, transcendentals=0)
OFFSETS = ((0, 0), (0, 1), (-1, 0), (-1, 1), (1, 0), (1, 1), (2, 0), (2, 1))


def shift_rep(value, steps):
    count = lax.axis_size("rep")
    return lax.ppermute(value, "rep", [(i, (i + steps) % count) for i in range(count)])


def shift_seq(value, dz, dy):
    pairs = []
    for z in range(Z):
        for y in range(Y):
            pairs.append((z * Y + y, (z + dz) % Z * Y + (y + dy) % Y))
    return lax.ppermute(value, "seq", pairs)


def member(me, dz, dy):
    z, y = me // Y, me % Y
    return lax.rem(z + dz + Z, Z) * Y + lax.rem(y + dy, Y)


def after(value, *others):
    return lax.optimization_barrier((value, *others))[0]


def gather_context(c, firsts, seconds):
    across = shift_seq(c, 0, 1)
    up, down = shift_seq(c, 1, 0), shift_seq(c, -1, 0)
    across, up, down, *_ = lax.optimization_barrier((across, up, down, *firsts))
    across_up, across_down = shift_seq(across, 1, 0), shift_seq(across, -1, 0)
    across_up, across_down, up, *_ = lax.optimization_barrier((across_up, across_down, up, *seconds))
    far, across_far = shift_seq(up, 1, 0), shift_seq(across_down, -1, 0)
    return (c, across, up, across_up, down, across_down, far, across_far)


def total(*terms):
    value = terms[0].astype(jnp.float32)
    for term in terms[1:]:
        value = value + term.astype(jnp.float32)
    return value.astype(jnp.bfloat16)


def scatter_sum(part, seconds, thirds):
    part = {offset: part[k] for k, offset in enumerate(OFFSETS)}
    a = shift_seq(part[2, 0], 1, 0)
    b = shift_seq(part[2, 1], -1, 0)
    a, b, *_ = lax.optimization_barrier((a, b, *seconds))
    u = shift_seq(jnp.stack([total(part[1, 0], a), part[1, 1]]), 1, 0)
    v = shift_seq(jnp.stack([part[-1, 0], total(part[-1, 1], b)]), -1, 0)
    u, v, *_ = lax.optimization_barrier((u, v, *thirds))
    there = total(part[0, 1], u[1], v[1])
    return (part[0, 0], u[0], v[0], shift_seq(there, 0, 1)), there


def part_kernel(factor, order, g_ref, w_ref, *refs):
    out_refs, g_all = refs[:-1], refs[-1]

    @pl.when(pl.program_id(0) == 0)
    def _():
        for k in range(g_ref.shape[0]):
            g_all[k] = g_ref[order[k]].T

    for k in range(g_ref.shape[0]):
        product = jnp.dot(g_all[k], w_ref[...], preferred_element_type=jnp.float32)
        out_refs[k][...] = (product * factor).astype(w_ref.dtype)


def part_blocks(order, g, w, factor):
    n, features, tokens = g.shape
    columns = w.shape[1]
    return pl.pallas_call(
        partial(part_kernel, factor),
        out_shape=(jax.ShapeDtypeStruct((tokens, columns), jnp.bfloat16),) * n,
        grid_spec=pltpu.PrefetchScalarGridSpec(
            num_scalar_prefetch=1,
            grid=(columns // UNIT,),
            in_specs=[
                pl.BlockSpec((n, features, tokens), lambda i, order: (0, 0, 0)),
                pl.BlockSpec((features, UNIT), lambda i, order: (0, i)),
            ],
            out_specs=(pl.BlockSpec((tokens, UNIT), lambda i, order: (0, i)),) * n,
            scratch_shapes=[pltpu.VMEM((n, tokens, features), jnp.bfloat16)],
        ),
        compiler_params=pltpu.CompilerParams(vmem_limit_bytes=14 << 20),
        cost_estimate=FREE,
    )(order, g, w)


def moved_kernel(factor, chunks, order, g_ref, mom_ref, *refs):
    n, features, tokens = g_ref.shape
    context_refs, out_refs, (g_all, rows) = refs[:n], refs[n:-2], refs[-2:]
    i = pl.program_id(0)

    @pl.when(i == 0)
    def _():
        for k in range(n):
            g_all[:, k * tokens : (k + 1) * tokens] = g_ref[order[k]]

    for k, ref in enumerate(context_refs):
        rows[k * tokens : (k + 1) * tokens, :] = ref[...]
    product = jnp.dot(g_all[...], rows[...], preferred_element_type=jnp.float32)
    value = (BETA * mom_ref[...].astype(jnp.float32) + product * factor).astype(mom_ref.dtype)
    first = 0
    for units, out_ref in zip(chunks, out_refs):

        @pl.when(jnp.logical_and(i >= first, i < first + units))
        def _():
            out_ref[...] = value

        first += units


def moved_chunks(order, g, mom, blocks, factor, start, chunks):
    n, features, tokens = g.shape
    specs = []
    first = 0
    for units in chunks:
        specs.append(
            pl.BlockSpec(
                (features, UNIT),
                lambda i, order, first=first, units=units: (0, jnp.clip(i - first, 0, units - 1)),
            )
        )
        first += units
    return pl.pallas_call(
        partial(moved_kernel, factor, chunks),
        out_shape=tuple(jax.ShapeDtypeStruct((features, units * UNIT), jnp.bfloat16) for units in chunks),
        grid_spec=pltpu.PrefetchScalarGridSpec(
            num_scalar_prefetch=1,
            grid=(first,),
            in_specs=[
                pl.BlockSpec((n, features, tokens), lambda i, order: (0, 0, 0)),
                pl.BlockSpec((features, UNIT), lambda i, order: (0, start + i)),
            ]
            + [pl.BlockSpec((tokens, UNIT), lambda i, order: (0, start + i))] * n,
            out_specs=tuple(specs),
            scratch_shapes=[
                pltpu.VMEM((features, n * tokens), jnp.bfloat16),
                pltpu.VMEM((n * tokens, UNIT), jnp.bfloat16),
            ],
        ),
        compiler_params=pltpu.CompilerParams(vmem_limit_bytes=18 << 20),
        cost_estimate=FREE,
    )(order, g, mom, *blocks)


def mix_kernel(w_ref, wq_ref, m_ref, mq_ref, *refs):
    nw_ref, nm_ref = refs[-2:]

    @pl.loop(0, w_ref.shape[0] // ROWS)
    def _(i):
        at = pl.ds(pl.multiple_of(i * ROWS, ROWS), ROWS)
        mixed = (m_ref[at, :].astype(jnp.float32) + mq_ref[at, :].astype(jnp.float32)) * 0.5
        both = (w_ref[at, :].astype(jnp.float32) + wq_ref[at, :].astype(jnp.float32)) * 0.5
        nw_ref[at, :] = (both - LEARN * mixed).astype(nw_ref.dtype)
        nm_ref[at, :] = mixed.astype(nm_ref.dtype)


def mix_chunk(w, wq, wq_start, m, mq, outs, start, units):
    features = w.shape[0]

    def at(first):
        return pl.BlockSpec((features, UNIT), lambda j: (0, first + j))

    shape = jax.ShapeDtypeStruct(w.shape, jnp.bfloat16)
    held = () if outs is None else tuple(outs)
    return pl.pallas_call(
        mix_kernel,
        out_shape=(shape, shape),
        grid=(units,),
        in_specs=[at(start), at(wq_start), at(0), at(0)] + [pl.BlockSpec(memory_space=pl.ANY)] * len(held),
        out_specs=(at(start), at(start)),
        input_output_aliases={4 + k: k for k in range(len(held))},
        compiler_params=pltpu.CompilerParams(vmem_limit_bytes=8 << 20),
        cost_estimate=FREE,
    )(w, wq, m, mq, *held)


def step(distance, back, idle_y, chunks, c, g, w, mom):
    factor = 1.0 / math.sqrt(c.shape[1])
    me = lax.axis_index("seq")
    order = jnp.stack([member(me, dz, dy) for dz, dy in OFFSETS]).astype(jnp.int32)
    n = Z * Y

    turned = g.T.reshape(n, g.shape[1] // n, g.shape[0])
    mine = lax.all_to_all(turned, "seq", split_axis=0, concat_axis=0, tiled=True)
    part = part_blocks(order, mine, w, factor)
    wide = back * UNIT
    if back:
        one = shift_rep(w[:, :wide], -distance)
        wq = shift_rep(w[:, wide:], distance)
        two = shift_rep(one, -distance)
        blocks = gather_context(c, (mine, one), (two, part[0]))
        wq_back = shift_rep(two, -distance)
        (m0,) = moved_chunks(order, mine, mom, blocks, factor, back, chunks[:1])
        (m_back,) = moved_chunks(after(order, m0), mine, mom, blocks, factor, 0, (back,))
        m1, m2 = moved_chunks(after(order, m_back), mine, mom, blocks, factor, back + chunks[0], chunks[1:])
        mq0, mq1, mq2 = shift_rep(m0, distance), shift_rep(m1, distance), shift_rep(m2, distance)
        first = shift_rep(m_back, -distance)
        second = shift_rep(first, -distance)
        mq_back = shift_rep(second, -distance)
        part = lax.optimization_barrier((*part, wq, wq_back, m2, mq0))[:n]
        terms, there = scatter_sum(part, (first,), (second, mq1))
        done = chunks[0]
        pieces = [
            [wq, 0, back, chunks[0], m0, mq0],
            [wq, done, back + done, chunks[1], m1, mq1],
            [wq_back, 0, 0, back, m_back, mq_back],
            [wq, done + chunks[1], back + done + chunks[1], chunks[2], m2, after(mq2, mq_back)],
        ]
    else:
        blocks = gather_context(c, (mine,), (part[0],))
        wq = shift_rep(w if idle_y else after(w, blocks[1]), distance)
        m = moved_chunks(order, mine, mom, blocks, factor, 0, chunks)
        mq = [shift_rep(chunk, distance) for chunk in m]
        part = lax.optimization_barrier((*part, m[-1], *((wq,) if idle_y else ())))[:n]
        terms, there = scatter_sum(part, mq[:1] if idle_y else (wq,), mq[1:2] if idle_y else ())
        pieces = []
        start = 0
        for k, units in enumerate(chunks):
            pieces.append([wq, start, start, units, m[k], mq[k]])
            start += units

    if idle_y:
        ctx_grad = total(*terms)
        pieces[-1][-1] = after(pieces[-1][-1], ctx_grad)
    else:
        pieces[0][-1] = after(pieces[0][-1], there)
        ctx_grad = total(*lax.optimization_barrier((*terms, pieces[-1][-1]))[:-1])
    outs = None
    for wq_part, wq_start, start, units, m_part, mq_part in pieces:
        outs = mix_chunk(w, wq_part, wq_start, m_part, mq_part, outs, start, units)
    return ctx_grad, outs[0], outs[1]


def local(context, grad_out, weight, momentum, gossip_round):
    level = jnp.remainder(gossip_round[0], 4)
    branches = [
        partial(step, 1, 0, False, (7, 6)),
        partial(step, 2, 0, False, (7, 6)),
        partial(step, 4, 3, True, (2, 5, 3)),
        partial(step, 8, 0, True, (5, 5, 3)),
    ]
    outs = lax.switch(level, branches, context[0], grad_out[0], weight[0], momentum[0])
    return tuple(out[None] for out in outs)


def solution(mesh):
    spec = P("rep", "seq", None)
    return jax.shard_map(
        local,
        mesh=mesh,
        in_specs=(spec, spec, spec, spec, P()),
        out_specs=(spec, spec, spec),
        check_vma=False,
    )
```

```python
from functools import partial
import math

import jax
import jax.numpy as jnp
from jax import lax
from jax.experimental import pallas as pl
from jax.experimental.pallas import tpu as pltpu
from jax.sharding import PartitionSpec as P

BETA = 0.9
LEARN = 0.1
UNIT = 256
ROWS = 64
Z, Y = 4, 2
FREE = pl.CostEstimate(flops=0, bytes_accessed=0, transcendentals=0)
OFFSETS = ((0, 0), (0, 1), (-1, 0), (-1, 1), (1, 0), (1, 1), (2, 0), (2, 1))


def shift_rep(value, steps):
    count = lax.axis_size("rep")
    return lax.ppermute(value, "rep", [(i, (i + steps) % count) for i in range(count)])


def shift_seq(value, dz, dy):
    pairs = []
    for z in range(Z):
        for y in range(Y):
            pairs.append((z * Y + y, (z + dz) % Z * Y + (y + dy) % Y))
    return lax.ppermute(value, "seq", pairs)


def member(me, dz, dy):
    z, y = me // Y, me % Y
    return lax.rem(z + dz + Z, Z) * Y + lax.rem(y + dy, Y)


def after(value, *others):
    return lax.optimization_barrier((value, *others))[0]


def turn_kernel(g_ref, out_ref):
    out_ref[...] = g_ref[...].T


def turn(g):
    tokens, features = g.shape
    wide = features // 2
    return pl.pallas_call(
        turn_kernel,
        out_shape=jax.ShapeDtypeStruct((features, tokens), g.dtype),
        grid=(features // wide,),
        in_specs=[pl.BlockSpec((tokens, wide), lambda i: (0, i))],
        out_specs=pl.BlockSpec((wide, tokens), lambda i: (i, 0)),
        compiler_params=pltpu.CompilerParams(vmem_limit_bytes=8 << 20),
        cost_estimate=FREE,
    )(g)


def gather_context(c, firsts, seconds):
    across = shift_seq(c, 0, 1)
    up, down = shift_seq(c, 1, 0), shift_seq(c, -1, 0)
    across, up, down, *_ = lax.optimization_barrier((across, up, down, *firsts))
    across_up, across_down = shift_seq(across, 1, 0), shift_seq(across, -1, 0)
    across_up, across_down, up, *_ = lax.optimization_barrier((across_up, across_down, up, *seconds))
    far, across_far = shift_seq(up, 1, 0), shift_seq(across_down, -1, 0)
    return (c, across, up, across_up, down, across_down, far, across_far)


def total(*terms):
    value = terms[0].astype(jnp.float32)
    for term in terms[1:]:
        value = value + term.astype(jnp.float32)
    return value.astype(jnp.bfloat16)


def scatter_sum(part, seconds, thirds):
    part = {offset: part[k] for k, offset in enumerate(OFFSETS)}
    a = shift_seq(part[2, 0], 1, 0)
    b = shift_seq(part[2, 1], -1, 0)
    a, b, *_ = lax.optimization_barrier((a, b, *seconds))
    u = shift_seq(jnp.stack([total(part[1, 0], a), part[1, 1]]), 1, 0)
    v = shift_seq(jnp.stack([part[-1, 0], total(part[-1, 1], b)]), -1, 0)
    u, v, *_ = lax.optimization_barrier((u, v, *thirds))
    there = total(part[0, 1], u[1], v[1])
    return (part[0, 0], u[0], v[0], shift_seq(there, 0, 1)), there


def part_kernel(factor, order, g_ref, w_ref, *refs):
    out_refs, g_all = refs[:-1], refs[-1]

    @pl.when(pl.program_id(0) == 0)
    def _():
        for k in range(g_ref.shape[0]):
            g_all[k] = g_ref[order[k]].T

    for k in range(g_ref.shape[0]):
        product = jnp.dot(g_all[k], w_ref[...], preferred_element_type=jnp.float32)
        out_refs[k][...] = (product * factor).astype(w_ref.dtype)


def part_blocks(order, g, w, factor):
    n, features, tokens = g.shape
    columns = w.shape[1]
    return pl.pallas_call(
        partial(part_kernel, factor),
        out_shape=(jax.ShapeDtypeStruct((tokens, columns), jnp.bfloat16),) * n,
        grid_spec=pltpu.PrefetchScalarGridSpec(
            num_scalar_prefetch=1,
            grid=(columns // UNIT,),
            in_specs=[
                pl.BlockSpec((n, features, tokens), lambda i, order: (0, 0, 0)),
                pl.BlockSpec((features, UNIT), lambda i, order: (0, i)),
            ],
            out_specs=(pl.BlockSpec((tokens, UNIT), lambda i, order: (0, i)),) * n,
            scratch_shapes=[pltpu.VMEM((n, tokens, features), jnp.bfloat16)],
        ),
        compiler_params=pltpu.CompilerParams(vmem_limit_bytes=14 << 20),
        cost_estimate=FREE,
    )(order, g, w)


def moved_kernel(factor, chunks, order, g_ref, mom_ref, *refs):
    n, features, tokens = g_ref.shape
    context_refs, out_refs, (g_all, rows) = refs[:n], refs[n:-2], refs[-2:]
    i = pl.program_id(0)

    @pl.when(i == 0)
    def _():
        for k in range(n):
            g_all[:, k * tokens : (k + 1) * tokens] = g_ref[order[k]]

    for k, ref in enumerate(context_refs):
        rows[k * tokens : (k + 1) * tokens, :] = ref[...]
    product = jnp.dot(g_all[...], rows[...], preferred_element_type=jnp.float32)
    value = (BETA * mom_ref[...].astype(jnp.float32) + product * factor).astype(mom_ref.dtype)
    first = 0
    for units, out_ref in zip(chunks, out_refs):

        @pl.when(jnp.logical_and(i >= first, i < first + units))
        def _():
            out_ref[...] = value

        first += units


def moved_chunks(order, g, mom, blocks, factor, start, chunks):
    n, features, tokens = g.shape
    specs = []
    first = 0
    for units in chunks:
        specs.append(
            pl.BlockSpec(
                (features, UNIT),
                lambda i, order, first=first, units=units: (0, jnp.clip(i - first, 0, units - 1)),
            )
        )
        first += units
    return pl.pallas_call(
        partial(moved_kernel, factor, chunks),
        out_shape=tuple(jax.ShapeDtypeStruct((features, units * UNIT), jnp.bfloat16) for units in chunks),
        grid_spec=pltpu.PrefetchScalarGridSpec(
            num_scalar_prefetch=1,
            grid=(first,),
            in_specs=[
                pl.BlockSpec((n, features, tokens), lambda i, order: (0, 0, 0)),
                pl.BlockSpec((features, UNIT), lambda i, order: (0, start + i)),
            ]
            + [pl.BlockSpec((tokens, UNIT), lambda i, order: (0, start + i))] * n,
            out_specs=tuple(specs),
            scratch_shapes=[
                pltpu.VMEM((features, n * tokens), jnp.bfloat16),
                pltpu.VMEM((n * tokens, UNIT), jnp.bfloat16),
            ],
        ),
        compiler_params=pltpu.CompilerParams(vmem_limit_bytes=18 << 20),
        cost_estimate=FREE,
    )(order, g, mom, *blocks)


def mix_kernel(w_ref, wq_ref, m_ref, mq_ref, *refs):
    nw_ref, nm_ref = refs[-2:]

    @pl.loop(0, w_ref.shape[0] // ROWS)
    def _(i):
        at = pl.ds(pl.multiple_of(i * ROWS, ROWS), ROWS)
        mixed = (m_ref[at, :].astype(jnp.float32) + mq_ref[at, :].astype(jnp.float32)) * 0.5
        both = (w_ref[at, :].astype(jnp.float32) + wq_ref[at, :].astype(jnp.float32)) * 0.5
        nw_ref[at, :] = (both - LEARN * mixed).astype(nw_ref.dtype)
        nm_ref[at, :] = mixed.astype(nm_ref.dtype)


def mix_chunk(w, wq, wq_start, m, mq, outs, start, units):
    features = w.shape[0]

    def at(first):
        return pl.BlockSpec((features, UNIT), lambda j: (0, first + j))

    shape = jax.ShapeDtypeStruct(w.shape, jnp.bfloat16)
    held = () if outs is None else tuple(outs)
    return pl.pallas_call(
        mix_kernel,
        out_shape=(shape, shape),
        grid=(units,),
        in_specs=[at(start), at(wq_start), at(0), at(0)] + [pl.BlockSpec(memory_space=pl.ANY)] * len(held),
        out_specs=(at(start), at(start)),
        input_output_aliases={4 + k: k for k in range(len(held))},
        compiler_params=pltpu.CompilerParams(vmem_limit_bytes=8 << 20),
        cost_estimate=FREE,
    )(w, wq, m, mq, *held)


def step(distance, back, idle_y, chunks, c, g, w, mom):
    factor = 1.0 / math.sqrt(c.shape[1])
    me = lax.axis_index("seq")
    order = jnp.stack([member(me, dz, dy) for dz, dy in OFFSETS]).astype(jnp.int32)
    n = Z * Y

    turned = turn(g).reshape(n, g.shape[1] // n, g.shape[0])
    mine = lax.all_to_all(turned, "seq", split_axis=0, concat_axis=0, tiled=True)
    part = part_blocks(order, mine, w, factor)
    wide = back * UNIT
    if back:
        one = shift_rep(w[:, :wide], -distance)
        wq = shift_rep(w[:, wide:], distance)
        two = shift_rep(one, -distance)
        blocks = gather_context(c, (mine, one), (two, part[0]))
        wq_back = shift_rep(two, -distance)
        (m0,) = moved_chunks(order, mine, mom, blocks, factor, back, chunks[:1])
        (m_back,) = moved_chunks(after(order, m0), mine, mom, blocks, factor, 0, (back,))
        m1, m2 = moved_chunks(after(order, m_back), mine, mom, blocks, factor, back + chunks[0], chunks[1:])
        mq0, mq1, mq2 = shift_rep(m0, distance), shift_rep(m1, distance), shift_rep(m2, distance)
        first = shift_rep(m_back, -distance)
        second = shift_rep(first, -distance)
        mq_back = shift_rep(second, -distance)
        part = lax.optimization_barrier((*part, wq, wq_back, m2, mq0))[:n]
        terms, there = scatter_sum(part, (first,), (second, mq1))
        done = chunks[0]
        pieces = [
            [wq, 0, back, chunks[0], m0, mq0],
            [wq, done, back + done, chunks[1], m1, mq1],
            [wq_back, 0, 0, back, m_back, mq_back],
            [wq, done + chunks[1], back + done + chunks[1], chunks[2], m2, after(mq2, mq_back)],
        ]
    else:
        blocks = gather_context(c, (mine,), (part[0],))
        wq = shift_rep(w if idle_y else after(w, blocks[1]), distance)
        m = moved_chunks(order, mine, mom, blocks, factor, 0, chunks)
        mq = [shift_rep(chunk, distance) for chunk in m]
        part = lax.optimization_barrier((*part, *((m[-1], wq) if idle_y else blocks[-2:])))[:n]
        terms, there = scatter_sum(part, mq[:1] if idle_y else (wq,), mq[1:2] if idle_y else ())
        pieces = []
        start = 0
        for k, units in enumerate(chunks):
            pieces.append([wq, start, start, units, m[k], mq[k]])
            start += units

    if idle_y:
        ctx_grad = total(*terms)
        for piece in pieces[-2:] if back else pieces[-1:]:
            piece[-1] = after(piece[-1], ctx_grad)
    else:
        pieces[0][-1] = after(pieces[0][-1], there)
        ctx_grad = total(*lax.optimization_barrier((*terms, pieces[-1][-1]))[:-1])
    outs = None
    for wq_part, wq_start, start, units, m_part, mq_part in pieces:
        outs = mix_chunk(w, wq_part, wq_start, m_part, mq_part, outs, start, units)
    return ctx_grad, outs[0], outs[1]


def local(context, grad_out, weight, momentum, gossip_round):
    level = jnp.remainder(gossip_round[0], 4)
    branches = [
        partial(step, 1, 0, False, (7, 6)),
        partial(step, 2, 0, False, (7, 6)),
        partial(step, 4, 3, True, (2, 5, 3)),
        partial(step, 8, 0, True, (5, 5, 3)),
    ]
    outs = lax.switch(level, branches, context[0], grad_out[0], weight[0], momentum[0])
    return tuple(out[None] for out in outs)


def solution(mesh):
    spec = P("rep", "seq", None)
    return jax.shard_map(
        local,
        mesh=mesh,
        in_specs=(spec, spec, spec, spec, P()),
        out_specs=(spec, spec, spec),
        check_vma=False,
    )
```
